256 devices in a mesh: img: 4 (over z_hi), exp: 64 (over x, z_lo, y, core).
Axes of the slice: x: 4, y: 4, z: 8 (z_hi: 4, z_lo: 2; z = z_hi * 2 + z_lo), core: 2. Of those that a mesh axis runs over, the one named last changes fastest.
Arguments:
- tokens: bfloat16 [3072, 64, 1280], P(('img', 'exp')), may hold values from -12 to 12
- router: bfloat16 [1280, 16], replicated, may hold values from -0.2 to 0.2
- grad_out: bfloat16 [3072, 64, 1280], P(('img', 'exp')), may hold values from -6 to 6
- slot_out: bfloat16 [3072, 16, 1280], P(('img', 'exp')), may hold values from -6 to 6
- hidden_pre: bfloat16 [3072, 64, 1280], P('img', 'exp'), may hold values from -6 to 6
- w_in: bfloat16 [64, 1280, 1280], P('exp', 'img'), may hold values from -0.15625 to 0.15625
- w_out: bfloat16 [64, 1280, 1280], P('exp', 'img'), may hold values from -0.078125 to 0.078125
Outputs:
- d_tokens: bfloat16 [3072, 64, 1280], P(('img', 'exp'))
- d_w_in: bfloat16 [64, 1280, 1280], P('exp', 'img')
- d_w_out: bfloat16 [64, 1280, 1280], P('exp', 'img')
- d_router: float32 [1280, 16], replicated
The draws below stay inside these ranges and needn't reach their ends.
All inputs are finite; a program needn't handle non-finite values.
Results may differ from the reference program's by a relative error of at most 0.015.
Values may be sent and summed in bfloat16 or wider, within the bound.
No kernel may reach another device: no remote copies, remote signals or barrier semaphores. Data moves between devices by JAX's collectives and lax.ppermute only.
A program may use at most 128 MiB of HBM per device.

```python
import jax
import jax.numpy as jnp
from jax import lax

D = 1280
FF = 5120
TOKS = 64
IMG_DEV = 12
SPLIT = 4
FQ = 1280
EXPERTS = 16
IMAGES = 3072
N_IMG = 4
N_EXP = 64


def router_parts(key):
    normal_part = jax.random.normal(jax.random.fold_in(key, 101), (D, EXPERTS), jnp.float32)
    return normal_part


def draw_router(key, part):
    normal_part = router_parts(key)
    values = jnp.clip(normal_part, -1.5, 1.5) * D ** (-0.5)
    return values.astype(jnp.bfloat16)


def draw_tokens(key, part):
    key = jax.random.fold_in(key, 5)
    values = jnp.clip(jax.random.normal(jax.random.fold_in(key, 1), (IMAGES, TOKS, D), jnp.float32), -6.0, 6.0)
    return values.astype(jnp.bfloat16)


def shard_levels(own_key, dims, shards, least, high):
    def one(axis_at, blocks):
        steps = jax.random.uniform(jax.random.fold_in(jax.random.fold_in(own_key, 6), axis_at), (blocks,), jnp.float32, least / len(shards), high / len(shards))
        return jnp.repeat(jnp.exp(steps), dims[axis_at] // blocks).reshape((-1,) + (1,) * (len(dims) - axis_at - 1))

    level = one(*shards[0])
    for cut in shards[1:]:
        level = level * one(*cut)
    return level


def gaussian(stream_key, extent, scale, most, shards=(), kind=jnp.bfloat16):
    entries = jax.random.normal(stream_key, extent, jnp.float32) * scale
    if len(shards) > 0:
        entries = shard_levels(stream_key, extent, shards, -0.22, 0.18) * entries
    return jnp.clip(entries, min=-most, max=most).astype(kind)


def setup_inputs(seed: int = 0) -> dict:
    keys = jax.random.split(jax.random.key(seed), 8)
    tokens = draw_tokens(jax.random.fold_in(keys[7], 71), 0)
    router = draw_router(jax.random.fold_in(keys[7], 71), 0)
    grad_out = gaussian(keys[2], (IMAGES, TOKS, D), 1.0, 6.0, ((0, 256),))
    slot_out = gaussian(keys[3], (IMAGES, EXPERTS, D), 1.0, 6.0, ((0, 256),))
    hidden_pre = gaussian(keys[4], (IMAGES, EXPERTS * SPLIT, FQ), 1.0, 6.0, ((0, 4), (1, 64)))
    w_in = gaussian(keys[5], (EXPERTS * SPLIT, D, FQ), D ** -0.5, 0.15625, ((0, 64), (1, 4)))
    w_out = gaussian(keys[6], (EXPERTS * SPLIT, FQ, D), FF ** -0.5, 0.078125, ((0, 64), (1, 4)))
    return {"tokens": tokens, "router": router, "grad_out": grad_out, "slot_out": slot_out, "hidden_pre": hidden_pre, "w_in": w_in, "w_out": w_out}


def gelu_tanh(values):
    return jax.nn.gelu(values, approximate=True)

def router_phase(block_tokens, router):
    logits = jnp.einsum('bmd,ds->bms', block_tokens.astype(jnp.float32), router.astype(jnp.float32))
    dispatch = jax.nn.softmax(logits, axis=1)
    combine = jax.nn.softmax(logits, axis=2)
    return (dispatch, combine)

def reference(tokens, router, grad_out, slot_out, hidden_pre, w_in, w_out):
    block_count = N_IMG * N_EXP
    token_blocks = tokens.reshape(block_count, IMG_DEV, TOKS, D)
    grad_blocks = grad_out.reshape(block_count, IMG_DEV, TOKS, D)
    output_blocks = slot_out.reshape(block_count, IMG_DEV, EXPERTS, D)

    def first_pass(bundle):
        block_tokens, block_grads = bundle
        dispatch, combine = router_phase(block_tokens, router)
        dispatch_w = dispatch.astype(jnp.bfloat16)
        combine_w = combine.astype(jnp.bfloat16)
        slot_inputs = jnp.einsum('bms,bmd->bsd', dispatch_w.astype(jnp.float32), block_tokens.astype(jnp.float32)).astype(jnp.bfloat16)
        slot_grads = jnp.einsum('bms,bmd->bsd', combine_w.astype(jnp.float32), block_grads.astype(jnp.float32)).astype(jnp.bfloat16)
        return (slot_inputs, slot_grads)
    slot_inputs, slot_grads = lax.map(first_pass, (token_blocks, grad_blocks))
    slot_inputs = slot_inputs.reshape(IMAGES, EXPERTS, D).transpose(1, 0, 2)
    slot_grads = slot_grads.reshape(IMAGES, EXPERTS, D).transpose(1, 0, 2)
    pre_parts = hidden_pre.reshape(IMAGES, EXPERTS, SPLIT, FQ).transpose(1, 2, 0, 3)
    in_parts = w_in.reshape(EXPERTS, SPLIT, D, FQ)
    out_parts = w_out.reshape(EXPERTS, SPLIT, FQ, D)

    def expert_pass(bundle):
        expert_inputs, expert_grads, expert_pre, expert_in, expert_out = bundle
        summed = jnp.zeros((IMAGES, D), jnp.float32)
        in_grads = []
        out_grads = []
        for member in range(SPLIT):
            activation, gelu_back = jax.vjp(gelu_tanh, expert_pre[member].astype(jnp.float32))
            activation = activation.astype(jnp.bfloat16)
            hidden_grad = jnp.dot(expert_grads, expert_out[member].T, preferred_element_type=jnp.float32)
            pre_grad = gelu_back(hidden_grad)[0].astype(jnp.bfloat16)
            out_grads.append(jnp.dot(activation.T, expert_grads, preferred_element_type=jnp.float32).astype(jnp.bfloat16))
            in_grads.append(jnp.dot(expert_inputs.T, pre_grad, preferred_element_type=jnp.float32).astype(jnp.bfloat16))
            summed = summed + jnp.dot(pre_grad, expert_in[member].T, preferred_element_type=jnp.float32)
        return (summed.astype(jnp.bfloat16), jnp.stack(in_grads), jnp.stack(out_grads))
    input_grads, d_w_in, d_w_out = lax.map(expert_pass, (slot_inputs, slot_grads, pre_parts, in_parts, out_parts))
    input_grads = input_grads.transpose(1, 0, 2).reshape(block_count, IMG_DEV, EXPERTS, D)

    def second_pass(bundle):
        block_tokens, block_grads, block_outputs, block_input_grads = bundle
        dispatch, combine = router_phase(block_tokens, router)
        dispatch_w = dispatch.astype(jnp.bfloat16)
        combine_grad = jnp.einsum('bmd,bsd->bms', block_grads.astype(jnp.float32), block_outputs.astype(jnp.float32))
        dispatch_grad = jnp.einsum('bmd,bsd->bms', block_tokens.astype(jnp.float32), block_input_grads.astype(jnp.float32))
        logit_grads = dispatch * (dispatch_grad - lax.optimization_barrier(jnp.sum(dispatch * dispatch_grad, axis=1, keepdims=True)))
        logit_grads = logit_grads + combine * (combine_grad - lax.optimization_barrier(jnp.sum(combine * combine_grad, axis=2, keepdims=True)))
        logit_grads = logit_grads.astype(jnp.bfloat16)
        token_grads = jnp.einsum('bms,ds->bmd', logit_grads.astype(jnp.float32), router.astype(jnp.float32))
        token_grads = token_grads + jnp.einsum('bms,bsd->bmd', dispatch_w.astype(jnp.float32), block_input_grads.astype(jnp.float32))
        router_piece = jnp.einsum('bmd,bms->ds', block_tokens.astype(jnp.float32), logit_grads.astype(jnp.float32))
        return (token_grads.astype(jnp.bfloat16), router_piece)
    d_tokens, router_terms = lax.map(second_pass, (token_blocks, grad_blocks, output_blocks, input_grads))
    return (d_tokens.reshape(IMAGES, TOKS, D), d_w_in.reshape(EXPERTS * SPLIT, D, FQ), d_w_out.reshape(EXPERTS * SPLIT, FQ, D), lax.optimization_barrier(jnp.sum(router_terms, axis=0)))
```

```python
import functools

import jax
import jax.numpy as jnp
from jax import lax
from jax.experimental import pallas as pl
from jax.experimental.pallas import tpu as pltpu
from jax.sharding import Mesh, PartitionSpec as P

BF16 = jnp.bfloat16
F32 = jnp.float32
IMG = ("zh1", "zh0")
EXP = ("x", "zl", "yh", "yl", "c")
AXES = IMG + EXP
EXPERT = ("x", "zl", "yh")
PAD = 16
VMEM_LIMIT = 48 * 1024 * 1024


def gelu_tanh(values):
    return jax.nn.gelu(values, approximate=True)


def dot(a, b, dims):
    return lax.dot_general(a, b, (dims, ((), ())), preferred_element_type=F32)


NN = ((1,), (0,))
NT = ((1,), (1,))
TN = ((0,), (0,))


def own_image(rows, columns, token_count):
    image = lax.broadcasted_iota(jnp.int32, (rows, columns), 0) // token_count
    return image == lax.broadcasted_iota(jnp.int32, (rows, columns), 1) % PAD


def front_kernel(token_count, tokens, grad_out, router, grads_out, inputs_out, dispatch_out, combine_out):
    rows = tokens.shape[0]
    columns = router.shape[1]
    images = rows // token_count
    logits = dot(tokens[...], router[...], NN)
    mine = own_image(rows, columns, token_count)
    weights = jnp.exp(logits - jnp.max(logits, axis=1, keepdims=True))
    weights = jnp.where(mine, weights, 0.0)
    combine = weights / jnp.sum(weights, axis=1, keepdims=True)
    grads_out[...] = dot(combine.astype(BF16), grad_out[...], TN).astype(BF16)
    combine_out[...] = combine
    by_image = logits.reshape(images, token_count, columns)
    weights = jnp.exp(by_image - jnp.max(by_image, axis=1, keepdims=True))
    dispatch = weights / jnp.sum(weights, axis=1, keepdims=True)
    dispatch = jnp.where(mine, dispatch.reshape(rows, columns), 0.0)
    inputs_out[...] = dot(dispatch.astype(BF16), tokens[...], TN).astype(BF16)
    dispatch_out[...] = dispatch


def combine_kernel(slot_count, grad_out, slot_out, combine, term_out):
    count = slot_out.shape[0]
    columns = combine.shape[1]
    row = lax.broadcasted_iota(jnp.int32, (columns, count), 0)
    source = lax.broadcasted_iota(jnp.int32, (columns, count), 1)
    order = (source == (row % PAD) * slot_count + row // PAD).astype(BF16)
    outputs = dot(order, slot_out[...], NN).astype(BF16)
    weights = combine[...]
    grads = weights * dot(grad_out[...], outputs, NT)
    term_out[...] = grads - weights * jnp.sum(grads, axis=1, keepdims=True)


def logit_kernel(token_count, slot_count, tokens, dispatch, term, input_grads, logit_out, router_out):
    rows, columns = dispatch.shape
    images = rows // token_count
    weights = dispatch[...]
    grads = weights * dot(tokens[...], input_grads[...], NT)
    total = jnp.sum(grads.reshape(images, token_count, columns), axis=1, keepdims=True)
    total = jnp.broadcast_to(total, (images, token_count, columns)).reshape(rows, columns)
    logit_grads = (grads - weights * total + term[...]).astype(BF16)
    logit_out[...] = logit_grads
    column = lax.broadcasted_iota(jnp.int32, (columns, slot_count), 0) // PAD
    fold = (column == lax.broadcasted_iota(jnp.int32, (columns, slot_count), 1)).astype(BF16)
    by_slot = dot(logit_grads, fold, NN).astype(BF16)
    router_out[...] = dot(by_slot, tokens[...], TN)


def token_kernel(dispatch, logit_grads, router, input_grads, tokens_out):
    total = dot(logit_grads[...], router[...], NT)
    total = total + dot(dispatch[...].astype(BF16), input_grads[...], NN)
    tokens_out[...] = total.astype(BF16)


def local_call(kernel, outs, *operands):
    whole = pl.BlockSpec(memory_space=pltpu.VMEM)
    return pl.pallas_call(
        kernel,
        out_shape=[jax.ShapeDtypeStruct(shape, dtype) for shape, dtype in outs],
        in_specs=[whole] * len(operands),
        out_specs=[whole] * len(outs),
        compiler_params=pltpu.CompilerParams(vmem_limit_bytes=VMEM_LIMIT),
    )(*operands)


def swap(values, axis, mask):
    count = lax.axis_size(axis)
    return lax.ppermute(values, axis, [(k, k ^ mask) for k in range(count)])


def to_image_pair(values):
    return swap(values, IMG, 3)


def to_weight_pair(values):
    return swap(values, IMG, 1)


def flip_blocks(blocks):
    zh1, zh0 = lax.axis_index("zh1"), lax.axis_index("zh0")
    blocks = [jnp.where(zh0 == 0, blocks[k], blocks[k ^ 1]) for k in range(4)]
    return [jnp.where(zh1 == 0, blocks[k], blocks[k ^ 2]) for k in range(4)]


def sum_everywhere(values):
    for axes in (("yl", "c"), ("x",), ("zl", "yh"), IMG):
        first, second, third = (swap(values, axes, mask) for mask in (1, 2, 3))
        values = (values + first) + (second + third)
    return values


def share(values):
    values = jnp.concatenate([values, swap(values, "yl", 1)])
    return jnp.concatenate([values, swap(values, "c", 1)])


def gather_share(values):
    half = values.shape[0] // 2
    values = values[:half] + swap(values[half:].astype(BF16), "c", 1).astype(F32)
    half = half // 2
    return values[:half] + swap(values[half:].astype(BF16), "yl", 1).astype(F32)


def on_device(tokens, router, grad_out, slot_out, hidden_pre, w_in, w_out):
    image_count, token_count, model_width = tokens.shape
    slot_count = router.shape[1]
    rows = image_count * token_count
    columns = slot_count * PAD
    group = slot_count * image_count
    zh1, zh0 = lax.axis_index("zh1"), lax.axis_index("zh0")
    yl, c = lax.axis_index("yl"), lax.axis_index("c")
    first_half = zh1 == 0

    hidden_pre = hidden_pre.reshape(-1, hidden_pre.shape[2])
    part = hidden_pre.shape[1] // 2
    pre_mine = jnp.where(first_half, hidden_pre[:, :part], hidden_pre[:, part:])
    pre_other = to_image_pair(jnp.where(first_half, hidden_pre[:, part:], hidden_pre[:, :part]))
    w_in, w_out = w_in[0], w_out[0]
    share_rows = w_in.shape[0]
    w_in_mine = jnp.where(first_half, w_in[:, :part], w_in[:, part:])
    w_in_pair = to_image_pair(jnp.where(first_half, w_in[:, part:], w_in[:, :part]))
    w_out_pair = to_weight_pair(w_out)

    tokens = tokens.reshape(rows, model_width)
    grad_out = grad_out.reshape(rows, model_width)
    router_wide = jnp.repeat(router, PAD, axis=1)
    slots = ((columns, model_width), BF16)
    wide = ((rows, columns), F32)
    slot_grads, slot_inputs, dispatch, combine = local_call(
        functools.partial(front_kernel, token_count),
        [slots, slots, wide, wide],
        tokens, grad_out, router_wide,
    )
    padded = lax.broadcasted_iota(jnp.int32, (group, columns), 1)
    row = lax.broadcasted_iota(jnp.int32, (group, columns), 0)
    pick = (padded == row // image_count * PAD + row % image_count).astype(BF16)

    def to_experts(values):
        values = lax.all_to_all(values, EXPERT, 0, 0, tiled=True)
        return dot(pick, values, NN).astype(BF16)

    slot_grads = to_experts(slot_grads)
    slot_grads_other = to_image_pair(slot_grads)
    slot_inputs = to_experts(slot_inputs)
    slot_inputs_other = to_image_pair(slot_inputs)
    grads_mine, grads_other = share(slot_grads), share(slot_grads_other)
    inputs_mine, inputs_other = share(slot_inputs), share(slot_inputs_other)

    (term,) = local_call(
        functools.partial(combine_kernel, slot_count), [wide],
        grad_out, slot_out.reshape(-1, model_width), combine,
    )

    count = hidden_pre.shape[0]
    place = lax.broadcasted_iota(jnp.int32, (count, count), 0)
    source = lax.broadcasted_iota(jnp.int32, (count, count), 1)
    member_c = (place // (2 * group)) ^ c
    member_y = (place // group % 2) ^ yl
    wanted = (place % group // image_count * 4 + member_y * 2 + member_c) * image_count + place % image_count
    order = (source == wanted).astype(BF16)
    pre_mine = dot(order, pre_mine, NN)
    pre_other = dot(order, pre_other, NN)

    w_out_half = jnp.where(
        zh0 == 0, jnp.concatenate([w_out, w_out_pair]), jnp.concatenate([w_out_pair, w_out])
    )
    w_in_both = to_weight_pair(jnp.concatenate([w_in_mine, w_in_pair]))
    w_in_half = jnp.concatenate(
        flip_blocks([w_in_mine, w_in_both[:share_rows], w_in_both[share_rows:], w_in_pair])
    )

    def expert(pre_values, grads):
        activation, gelu_back = jax.vjp(gelu_tanh, pre_values)
        hidden_grad = dot(grads, w_out_half, NT)
        pre_grad = gelu_back(hidden_grad)[0].astype(BF16)
        return activation.astype(BF16), pre_grad

    act_other, pre_grad_other = expert(pre_other, grads_other)
    act_mine, pre_grad_mine = expert(pre_mine, grads_mine)
    back_other = gather_share(dot(pre_grad_other, w_in_half, NT))
    back_other = to_image_pair(back_other.astype(BF16))
    back_mine = gather_share(dot(pre_grad_mine, w_in_half, NT))
    back = (back_mine + back_other.astype(F32)).astype(BF16)
    back = dot(pick, back, TN).astype(BF16)
    input_grads = lax.all_to_all(back, EXPERT, 0, 0, tiled=True)

    logit_grads, router_grads = local_call(
        functools.partial(logit_kernel, token_count, slot_count),
        [((rows, columns), BF16), ((slot_count, model_width), F32)],
        tokens, dispatch, term, input_grads,
    )
    router_total = sum_everywhere(router_grads)
    (token_grads,) = local_call(
        token_kernel, [((rows, model_width), BF16)],
        dispatch, logit_grads, router_wide, input_grads,
    )

    out_partial = dot(act_other, grads_other, TN) + dot(act_mine, grads_mine, TN)
    out_first, out_second = out_partial[:share_rows], out_partial[share_rows:]
    out_sent = jnp.where(zh0 == 0, out_second, out_first).astype(BF16)
    out_gradient = jnp.where(zh0 == 0, out_first, out_second)
    out_gradient = (out_gradient + to_weight_pair(out_sent).astype(F32)).astype(BF16)

    in_partial = dot(inputs_other, pre_grad_other, TN) + dot(inputs_mine, pre_grad_mine, TN)
    blocks = flip_blocks([in_partial[k * share_rows:(k + 1) * share_rows] for k in range(4)])
    in_arrived = to_weight_pair(jnp.concatenate([blocks[1], blocks[2]]).astype(BF16)).astype(F32)
    in_mine = (blocks[0] + in_arrived[:share_rows]).astype(BF16)
    in_pair = to_image_pair((blocks[3] + in_arrived[share_rows:]).astype(BF16))
    in_gradient = jnp.where(
        first_half,
        jnp.concatenate([in_mine, in_pair], axis=1),
        jnp.concatenate([in_pair, in_mine], axis=1),
    )
    return (
        token_grads.reshape(image_count, token_count, model_width),
        in_gradient[None],
        out_gradient[None],
        router_total.T,
    )


def solution(mesh):
    fine = Mesh(mesh.devices.reshape(2, 2, 4, 2, 2, 2, 2), AXES)
    in_specs = (
        P(AXES, None, None),
        P(),
        P(AXES, None, None),
        P(AXES, None, None),
        P(IMG, EXP, None),
        P(EXP, IMG, None),
        P(EXP, IMG, None),
    )
    out_specs = (P(AXES, None, None), P(EXP, IMG, None), P(EXP, IMG, None), P())
    return jax.shard_map(
        on_device, mesh=fine, in_specs=in_specs, out_specs=out_specs, check_vma=False
    )
```

```python
import functools

import jax
import jax.numpy as jnp
from jax import lax
from jax.experimental import pallas as pl
from jax.experimental.pallas import tpu as pltpu
from jax.sharding import Mesh, PartitionSpec as P

BF16 = jnp.bfloat16
F32 = jnp.float32
IMG = ("zh1", "zh0")
EXP = ("x", "zl", "yh", "yl", "c")
AXES = IMG + EXP
EXPERT = ("x", "zl", "yh")
PAD = 16
VMEM_LIMIT = 26 * 1024 * 1024
CUBIC = 0.044715
SLOPE = 0.7978845608028654


def dot(a, b, dims):
    return lax.dot_general(a, b, (dims, ((), ())), preferred_element_type=F32)


NN = ((1,), (0,))
NT = ((1,), (1,))
TN = ((0,), (0,))


def row_index(count):
    return lax.broadcasted_iota(jnp.int32, (count, 1), 0)


def one_hot(wanted, width):
    return (lax.broadcasted_iota(jnp.int32, (wanted.shape[0], width), 1) == wanted).astype(BF16)


def own_image(rows, columns, token_count):
    image = lax.broadcasted_iota(jnp.int32, (1, columns), 1) % PAD
    return row_index(rows) // token_count == image


def widen(router):
    slot_count = router.shape[1]
    slot = lax.broadcasted_iota(jnp.int32, (slot_count, slot_count * PAD), 0)
    column = lax.broadcasted_iota(jnp.int32, (slot_count, slot_count * PAD), 1)
    return dot(router[...], (column // PAD == slot).astype(BF16), NN).astype(BF16)


def spread_columns(columns, width, image_count, start):
    row = row_index(columns)
    column = row // PAD * (2 * image_count) + row % PAD + start
    return one_hot(jnp.where(row % PAD < image_count, column, width), width)


def front_kernel(token_count, tokens, grad_out, router, slots_out, combine_out, dispatch_out):
    rows, columns = combine_out.shape
    image_count = rows // token_count
    width = slots_out.shape[0]
    logits = dot(tokens[...], widen(router), NN)
    mine = own_image(rows, columns, token_count)
    weights = jnp.exp(logits - jnp.max(logits, axis=1, keepdims=True))
    weights = jnp.where(mine, weights, 0.0)
    combine = weights / jnp.sum(weights, axis=1, keepdims=True)
    weights = dot(combine.astype(BF16), spread_columns(columns, width, image_count, 0), NN)
    slots = dot(weights.astype(BF16), grad_out[...], TN)
    combine_out[...] = combine
    by_image = logits.reshape(rows // token_count, token_count, columns)
    weights = jnp.exp(by_image - jnp.max(by_image, axis=1, keepdims=True))
    dispatch = weights / jnp.sum(weights, axis=1, keepdims=True)
    dispatch = jnp.where(mine, dispatch.reshape(rows, columns), 0.0)
    order = spread_columns(columns, width, image_count, image_count)
    weights = dot(dispatch.astype(BF16), order, NN)
    slots_out[...] = (slots + dot(weights.astype(BF16), tokens[...], TN)).astype(BF16)
    dispatch_out[...] = dispatch


def combine_kernel(slot_count, grad_out, slot_out, combine, term_out):
    row = row_index(combine.shape[1])
    order = one_hot(row % PAD * slot_count + row // PAD, slot_out.shape[0])
    order = jnp.where(row % PAD < slot_out.shape[0] // slot_count, order, jnp.zeros_like(order))
    outputs = dot(order, slot_out[...], NN).astype(BF16)
    weights = combine[...]
    grads = weights * dot(grad_out[...], outputs, NT)
    term_out[...] = grads - weights * jnp.sum(grads, axis=1, keepdims=True)


def logit_kernel(token_count, slot_count, tokens, dispatch, term, input_grads, logit_out, router_out):
    rows, columns = dispatch.shape
    images = rows // token_count
    weights = dispatch[...]
    grads = weights * dot(tokens[...], input_grads[...], NT)
    total = jnp.sum(grads.reshape(images, token_count, columns), axis=1, keepdims=True)
    total = jnp.broadcast_to(total, (images, token_count, columns)).reshape(rows, columns)
    logit_grads = (grads - weights * total + term[...]).astype(BF16)
    logit_out[...] = logit_grads
    fold = one_hot(row_index(columns) // PAD, slot_count)
    by_slot = dot(logit_grads, fold, NN).astype(BF16)
    router_out[...] = dot(by_slot, tokens[...], TN)


def token_kernel(dispatch, logit_grads, router, input_grads, tokens_out):
    total = dot(logit_grads[...], widen(router), NT)
    total = total + dot(dispatch[...].astype(BF16), input_grads[...], NN)
    tokens_out[...] = total.astype(BF16)


def orders(image_count, group, place, count):
    row = row_index(group)
    base = row // image_count * (4 * image_count) + row % image_count
    for piece in range(4):
        member = ((piece % 2) ^ place[2]) * 2 + ((piece // 2) ^ place[3])
        rows = slice(piece * group, (piece + 1) * group)
        yield rows, one_hot(base + member * image_count, count)


def order_mine_kernel(image_count, group, place, hidden_pre, mine_out):
    half = mine_out.shape[1]
    values = jnp.where(place[0] == 0, hidden_pre[:, :half], hidden_pre[:, half:])
    for rows, order in orders(image_count, group, place, hidden_pre.shape[0]):
        mine_out[rows] = dot(order, values, NN).astype(BF16)


def order_other_kernel(image_count, group, place, first, second, other_out):
    count = first.shape[0]
    for rows, order in orders(image_count, group, place, 2 * count):
        other = dot(order[:, :count], first[...], NN) + dot(order[:, count:], second[...], NN)
        other_out[rows] = other.astype(BF16)


def pass_kernel(values, values_out):
    values_out[...] = values[:values_out.shape[0]]


def stack_kernel(first, second, stacked_out):
    stack(stacked_out, (first, second))


def stack(target, sources):
    start = 0
    for source in sources:
        count = source.shape[0]
        target[start:start + count] = source[...]
        start += count


def pick_rows(image_count, group):
    row = row_index(group)
    return one_hot(row // image_count * PAD + row % image_count, group // image_count * PAD)


def pick_kernel(image_count, values, grads_out, inputs_out):
    row = row_index(grads_out.shape[0])
    source = row // image_count * (2 * image_count) + row % image_count
    count = values.shape[0]
    grads_out[...] = dot(one_hot(source, count), values[...], NN).astype(BF16)
    inputs_out[...] = dot(one_hot(source + image_count, count), values[...], NN).astype(BF16)


def add_kernel(keep, arrived, keep_out, send_out):
    total = keep[...] + arrived[...].astype(F32)
    rows = keep_out.shape[0]
    keep_out[...], send_out[...] = total[:rows], total[rows:].astype(BF16)


def join_kernel(mine, arrived, sum_out):
    sum_out[...] = (mine[...] + arrived[...].astype(F32)).astype(BF16)


def spread_kernel(image_count, mine, other, spread_out):
    total = (mine[...] + other[...].astype(F32)).astype(BF16)
    spread_out[...] = dot(pick_rows(image_count, mine.shape[0]), total, TN).astype(BF16)


def expert_kernel(*refs):
    pre, w_out, w_in, act_out, grad_out, keep_out, send_out, grads = refs[-8:]
    stack(grads, refs[:-8])
    half = grads.shape[0] // 2
    for part in (0, 1):
        rows = slice(part * half, (part + 1) * half)
        hidden_grad = dot(grads[rows], w_out[...], NT)
        values = pre[rows].astype(F32)
        square = values * values
        bend = jnp.tanh(values * (SLOPE + SLOPE * CUBIC * square))
        step = 0.5 + 0.5 * bend
        act_out[rows] = (values * step).astype(BF16)
        slope = step + values * (0.5 - 0.5 * bend * bend) * (SLOPE + 3.0 * SLOPE * CUBIC * square)
        pre_grad = (hidden_grad * slope).astype(BF16)
        grad_out[rows] = pre_grad
        back = dot(pre_grad, w_in[...], NT)
        if part == 0:
            keep_out[...] = back
        else:
            send_out[...] = back.astype(BF16)


def out_weight_kernel(place, act_mine, act_other, *refs):
    keep_out, early_out, late_out, left, right = refs[-5:]
    stack(left, (act_mine, act_other))
    stack(right, refs[:-5])
    rows = keep_out.shape[0]
    zh0 = place[1]
    total = dot(left[...], right[...], TN)
    first, second = total[:rows], total[rows:]
    keep_out[...] = jnp.where(zh0 == 0, first, second)
    send = jnp.where(zh0 == 0, second, first).astype(BF16)
    early_out[...], late_out[...] = send[:rows // 2], send[rows // 2:]


def in_weight_kernel(place, grad_mine, grad_other, *refs):
    mine_out, pair_out, early_out, late_out, left, right, total = refs[-7:]
    stack(right, (grad_mine, grad_other))
    stack(left, refs[:-7])
    rows = mine_out.shape[0]
    position = place[0] * 2 + place[1]
    total[...] = dot(left[...], right[...], TN)

    def block(relative):
        return total[pl.ds(pl.multiple_of((position ^ relative) * rows, rows), rows)]

    mine_out[...], pair_out[...] = block(0), block(3)
    early_out[...], late_out[...] = block(2).astype(BF16), block(1).astype(BF16)


def sum_kernel(first, second, third, fourth, sum_out):
    sum_out[...] = (first[...] + second[...]) + (third[...] + fourth[...])


def local_call(kernel, outs, *operands, place=None, later_than=(), scratch=()):
    whole = pl.BlockSpec(memory_space=pltpu.VMEM)
    scalars = [] if place is None else [place]
    used = len(scalars) + len(operands)
    late = len(later_than)

    def body(*refs):
        kernel(*refs[:used], *refs[used + late:])

    return pl.pallas_call(
        body,
        out_shape=[jax.ShapeDtypeStruct(shape, dtype) for shape, dtype in outs],
        in_specs=[pl.BlockSpec(memory_space=pltpu.SMEM)] * len(scalars)
        + [whole] * len(operands)
        + [pl.BlockSpec(memory_space=pl.ANY)] * late,
        out_specs=[whole] * len(outs),
        scratch_shapes=[pltpu.VMEM(shape, dtype) for shape, dtype in scratch],
        compiler_params=pltpu.CompilerParams(vmem_limit_bytes=VMEM_LIMIT),
        cost_estimate=pl.CostEstimate(flops=0, bytes_accessed=0, transcendentals=0),
    )(*scalars, *operands, *later_than)


def swap(values, axis, mask):
    count = lax.axis_size(axis)
    return lax.ppermute(values, axis, [(k, k ^ mask) for k in range(count)])


def to_image_pair(values):
    return swap(values, IMG, 3)


def to_weight_pair(values):
    return swap(values, IMG, 1)


def flip_blocks(blocks):
    zh1, zh0 = lax.axis_index("zh1"), lax.axis_index("zh0")
    blocks = [jnp.where(zh0 == 0, blocks[k], blocks[k ^ 1]) for k in range(4)]
    return [jnp.where(zh1 == 0, blocks[k], blocks[k ^ 2]) for k in range(4)]


def sum_round(values, axes, later_than=()):
    moved = [swap(values, axes, mask) for mask in (1, 2, 3)]
    return local_call(
        sum_kernel, [(values.shape, values.dtype)], values, *moved, later_than=later_than
    )[0]


def share(values):
    joined = jnp.concatenate([values, swap(values, "yl", 1)])
    return joined, swap(joined, "c", 1)


def gather_share(keep, send):
    values = keep + swap(send, "c", 1).astype(F32)
    half = values.shape[0] // 2
    return values[:half] + swap(values[half:].astype(BF16), "yl", 1).astype(F32)


def on_device(tokens, router, grad_out, slot_out, hidden_pre, w_in, w_out):
    image_count, token_count, model_width = tokens.shape
    slot_count = router.shape[1]
    rows = image_count * token_count
    columns = slot_count * PAD
    group = slot_count * image_count
    zh1, zh0 = lax.axis_index("zh1"), lax.axis_index("zh0")
    place = jnp.stack([lax.axis_index(name) for name in ("zh1", "zh0", "yl", "c")])
    first_half = zh1 == 0

    hidden_pre = hidden_pre.reshape(-1, hidden_pre.shape[2])
    part = hidden_pre.shape[1] // 2
    w_in, w_out = w_in[0], w_out[0]
    share_rows = w_in.shape[0]
    w_in_mine = jnp.where(first_half, w_in[:, :part], w_in[:, part:])
    w_in_pair = to_image_pair(jnp.where(first_half, w_in[:, part:], w_in[:, :part]))
    w_out_pair = to_weight_pair(w_out)
    pre_sent = jnp.where(first_half, hidden_pre[:, part:], hidden_pre[:, :part])
    pre_early = to_image_pair(pre_sent[:2 * group])
    pre_late = to_image_pair(pre_sent[2 * group:])

    tokens = tokens.reshape(rows, model_width)
    grad_out = grad_out.reshape(rows, model_width)
    slots = ((columns, model_width), BF16)
    picked = ((group, model_width), BF16)
    wide = ((rows, columns), F32)
    slot_values, combine, dispatch = local_call(
        functools.partial(front_kernel, token_count),
        [((2 * group, model_width), BF16), wide, wide],
        tokens, grad_out, router,
    )
    slot_values_moved = lax.all_to_all(slot_values, EXPERT, 0, 0, tiled=True)
    (term,) = local_call(
        functools.partial(combine_kernel, slot_count), [wide],
        grad_out, slot_out.reshape(-1, model_width), combine,
        later_than=(slot_values,),
    )
    w_in_near = to_weight_pair(w_in_mine)
    grads_own, inputs_own = local_call(
        functools.partial(pick_kernel, image_count), [picked, picked],
        slot_values_moved, later_than=(term, pre_early, w_in_pair, w_out_pair, w_in_near),
    )
    grads_pair = to_image_pair(grads_own)
    grads_mine = share(grads_own)
    inputs_mine = share(inputs_own)
    w_in_far = to_weight_pair(w_in_pair)
    (grads_pair,) = local_call(
        pass_kernel, [picked], grads_pair, later_than=(w_in_far, grads_mine[0])
    )
    grads_other = share(grads_pair)
    w_out_half = jnp.where(
        zh0 == 0, jnp.concatenate([w_out, w_out_pair]), jnp.concatenate([w_out_pair, w_out])
    )
    w_in_half = jnp.concatenate(
        flip_blocks([w_in_mine, w_in_near, w_in_far, w_in_pair])
    )
    expert_outs = [
        ((4 * group, part), BF16),
        ((4 * group, part), BF16),
        ((2 * group, model_width), F32),
        ((2 * group, model_width), BF16),
    ]
    expert_scratch = [((4 * group, model_width), BF16)]
    half_pre = ((4 * group, part), BF16)
    (pre_mine,) = local_call(
        functools.partial(order_mine_kernel, image_count, group), [half_pre],
        hidden_pre,
        place=place, later_than=(grads_pair,),
    )
    act_mine, pre_grad_mine, keep_mine, send_mine = local_call(
        expert_kernel, expert_outs,
        *grads_mine, pre_mine, w_out_half, w_in_half,
        later_than=(grads_other[0],), scratch=expert_scratch,
    )
    (pre_other,) = local_call(
        functools.partial(order_other_kernel, image_count, group), [half_pre],
        pre_early, pre_late,
        place=place, later_than=(act_mine, inputs_mine[0]),
    )
    act_other, pre_grad_other, keep_other, send_other = local_call(
        expert_kernel, expert_outs,
        *grads_other, pre_other, w_out_half, w_in_half,
        later_than=(act_mine,), scratch=expert_scratch,
    )
    back_mine = gather_share(keep_mine, send_mine)
    out_keep, out_early, out_late = local_call(
        out_weight_kernel,
        [((share_rows, model_width), F32)] + [((share_rows // 2, model_width), BF16)] * 2,
        act_mine, act_other, *grads_mine, *grads_other,
        place=place, later_than=(send_other,),
        scratch=[((8 * group, part), BF16), ((8 * group, model_width), BF16)],
    )
    out_early, out_late = to_weight_pair(out_early), to_weight_pair(out_late)

    (inputs_sent,) = local_call(pass_kernel, [picked], inputs_own, later_than=(pre_late,))
    inputs_pair = to_image_pair(inputs_sent)

    half_sum, half_sent = local_call(
        add_kernel, [((group, model_width), F32), picked],
        keep_other, swap(send_other, "c", 1), later_than=(out_keep,),
    )
    (back_other,) = local_call(
        join_kernel, [picked],
        half_sum, swap(half_sent, "yl", 1), later_than=(inputs_pair, out_early),
    )
    back_pair = to_image_pair(back_other)
    (inputs_pair,) = local_call(
        pass_kernel, [picked], inputs_pair, later_than=(back_other,)
    )
    (inputs_joined,) = local_call(
        stack_kernel, [((2 * group, model_width), BF16)],
        inputs_pair, swap(inputs_pair, "yl", 1), later_than=(back_pair,),
    )
    inputs_other = inputs_joined, swap(inputs_joined, "c", 1)

    in_mine, in_pair, in_early, in_late = local_call(
        in_weight_kernel,
        [((share_rows, part), F32)] * 2 + [((share_rows, part), BF16)] * 2,
        pre_grad_mine, pre_grad_other, *inputs_mine, *inputs_other,
        place=place, later_than=(out_keep,),
        scratch=[
            ((8 * group, model_width), BF16), ((8 * group, part), BF16), ((model_width, part), F32),
        ],
    )
    in_early = to_weight_pair(in_early)
    (back,) = local_call(
        functools.partial(spread_kernel, image_count), [slots],
        back_mine, back_pair, later_than=(out_late,),
    )
    input_grads = lax.all_to_all(back, EXPERT, 0, 0, tiled=True)
    logit_grads, router_grads = local_call(
        functools.partial(logit_kernel, token_count, slot_count),
        [((rows, columns), BF16), ((slot_count, model_width), F32)],
        tokens, dispatch, term, input_grads, later_than=(in_mine,),
    )
    (token_grads,) = local_call(
        token_kernel, [((rows, model_width), BF16)],
        dispatch, logit_grads, router, input_grads,
    )
    (in_pair_sum,) = local_call(join_kernel, [((share_rows, part), BF16)], in_pair, in_early)
    (in_late,) = local_call(
        pass_kernel, [((share_rows, part), BF16)], in_late, later_than=(in_pair_sum,)
    )
    in_late = to_weight_pair(in_late)
    in_pair = to_image_pair(in_pair_sum)
    router_sum = sum_round(router_grads, ("yl", "c"), later_than=(token_grads,))
    router_sum = sum_round(router_sum, ("x",), later_than=(in_pair_sum,))
    router_sum = sum_round(router_sum, ("zl", "yh"), later_than=(in_pair,))
    router_sum = sum_round(router_sum, IMG)
    (in_mine,) = local_call(join_kernel, [((share_rows, part), BF16)], in_mine, in_late)
    out_arrived = jnp.concatenate([out_early, out_late])
    out_gradient = (out_keep + out_arrived.astype(F32)).astype(BF16)
    in_gradient = jnp.where(
        first_half,
        jnp.concatenate([in_mine, in_pair], axis=1),
        jnp.concatenate([in_pair, in_mine], axis=1),
    )
    return (
        token_grads.reshape(image_count, token_count, model_width),
        in_gradient[None],
        out_gradient[None],
        router_sum.T,
    )


def solution(mesh):
    fine = Mesh(mesh.devices.reshape(2, 2, 4, 2, 2, 2, 2), AXES)
    in_specs = (
        P(AXES, None, None),
        P(),
        P(AXES, None, None),
        P(AXES, None, None),
        P(IMG, EXP, None),
        P(EXP, IMG, None),
        P(EXP, IMG, None),
    )
    out_specs = (P(AXES, None, None), P(EXP, IMG, None), P(EXP, IMG, None), P())
    return jax.shard_map(
        on_device, mesh=fine, in_specs=in_specs, out_specs=out_specs, check_vma=False
    )
```

```python
import functools

import jax
import jax.numpy as jnp
from jax import lax
from jax.experimental import pallas as pl
from jax.experimental.pallas import tpu as pltpu
from jax.sharding import Mesh, PartitionSpec as P

BF16 = jnp.bfloat16
F32 = jnp.float32
IMG = ("zh1", "zh0")
EXP = ("x", "zl", "yh", "yl", "c")
AXES = IMG + EXP
EXPERT = ("x", "zl", "yh")
PAD = 16
VMEM_LIMIT = 26 * 1024 * 1024
CUBIC = 0.044715
SLOPE = 0.7978845608028654


def dot(a, b, dims):
    return lax.dot_general(a, b, (dims, ((), ())), preferred_element_type=F32)


NN = ((1,), (0,))
NT = ((1,), (1,))
TN = ((0,), (0,))


def row_index(count):
    return lax.broadcasted_iota(jnp.int32, (count, 1), 0)


def one_hot(wanted, width):
    return (lax.broadcasted_iota(jnp.int32, (wanted.shape[0], width), 1) == wanted).astype(BF16)


def own_image(rows, columns, token_count):
    image = lax.broadcasted_iota(jnp.int32, (1, columns), 1) % PAD
    return row_index(rows) // token_count == image


def widen(router):
    slot_count = router.shape[1]
    slot = lax.broadcasted_iota(jnp.int32, (slot_count, slot_count * PAD), 0)
    column = lax.broadcasted_iota(jnp.int32, (slot_count, slot_count * PAD), 1)
    return dot(router[...], (column // PAD == slot).astype(BF16), NN).astype(BF16)


def spread_columns(columns, width, image_count, start):
    row = row_index(columns)
    column = row // PAD * (2 * image_count) + row % PAD + start
    return one_hot(jnp.where(row % PAD < image_count, column, width), width)


def front_kernel(token_count, tokens, grad_out, router, slots_out, combine_out, dispatch_out):
    rows, columns = combine_out.shape
    image_count = rows // token_count
    width = slots_out.shape[0]
    logits = dot(tokens[...], widen(router), NN)
    mine = own_image(rows, columns, token_count)
    weights = jnp.exp(logits - jnp.max(logits, axis=1, keepdims=True))
    weights = jnp.where(mine, weights, 0.0)
    combine = weights / jnp.sum(weights, axis=1, keepdims=True)
    weights = dot(combine.astype(BF16), spread_columns(columns, width, image_count, 0), NN)
    slots = dot(weights.astype(BF16), grad_out[...], TN)
    combine_out[...] = combine
    by_image = logits.reshape(rows // token_count, token_count, columns)
    weights = jnp.exp(by_image - jnp.max(by_image, axis=1, keepdims=True))
    dispatch = weights / jnp.sum(weights, axis=1, keepdims=True)
    dispatch = jnp.where(mine, dispatch.reshape(rows, columns), 0.0)
    order = spread_columns(columns, width, image_count, image_count)
    weights = dot(dispatch.astype(BF16), order, NN)
    slots_out[...] = (slots + dot(weights.astype(BF16), tokens[...], TN)).astype(BF16)
    dispatch_out[...] = dispatch


def combine_kernel(slot_count, grad_out, slot_out, combine, term_out):
    row = row_index(combine.shape[1])
    order = one_hot(row % PAD * slot_count + row // PAD, slot_out.shape[0])
    order = jnp.where(row % PAD < slot_out.shape[0] // slot_count, order, jnp.zeros_like(order))
    outputs = dot(order, slot_out[...], NN).astype(BF16)
    weights = combine[...]
    grads = weights * dot(grad_out[...], outputs, NT)
    term_out[...] = grads - weights * jnp.sum(grads, axis=1, keepdims=True)


def logit_kernel(token_count, slot_count, tokens, dispatch, term, input_grads, logit_out, router_out):
    rows, columns = dispatch.shape
    images = rows // token_count
    weights = dispatch[...]
    grads = weights * dot(tokens[...], input_grads[...], NT)
    total = jnp.sum(grads.reshape(images, token_count, columns), axis=1, keepdims=True)
    total = jnp.broadcast_to(total, (images, token_count, columns)).reshape(rows, columns)
    logit_grads = (grads - weights * total + term[...]).astype(BF16)
    logit_out[...] = logit_grads
    fold = one_hot(row_index(columns) // PAD, slot_count)
    by_slot = dot(logit_grads, fold, NN).astype(BF16)
    router_out[...] = dot(by_slot, tokens[...], TN).astype(router_out.dtype)


def token_kernel(dispatch, logit_grads, router, input_grads, tokens_out):
    total = dot(logit_grads[...], widen(router), NT)
    total = total + dot(dispatch[...].astype(BF16), input_grads[...], NN)
    tokens_out[...] = total.astype(BF16)


def orders(image_count, group, place, count):
    row = row_index(group)
    base = row // image_count * (4 * image_count) + row % image_count
    for piece in range(4):
        member = ((piece % 2) ^ place[2]) * 2 + ((piece // 2) ^ place[3])
        rows = slice(piece * group, (piece + 1) * group)
        yield rows, one_hot(base + member * image_count, count)


def order_mine_kernel(image_count, group, place, hidden_pre, mine_out):
    half = mine_out.shape[1]
    values = jnp.where(place[0] == 0, hidden_pre[:, :half], hidden_pre[:, half:])
    for rows, order in orders(image_count, group, place, hidden_pre.shape[0]):
        mine_out[rows] = dot(order, values, NN).astype(BF16)


def order_other_kernel(image_count, group, place, first, second, other_out):
    count = first.shape[0]
    for rows, order in orders(image_count, group, place, count + second.shape[0]):
        other = dot(order[:, :count], first[...], NN) + dot(order[:, count:], second[...], NN)
        other_out[rows] = other.astype(BF16)


def pass_kernel(values, values_out):
    values_out[...] = values[:values_out.shape[0]]


def stack_kernel(first, second, stacked_out):
    stack(stacked_out, (first, second))


def stack(target, sources):
    start = 0
    for source in sources:
        count = source.shape[0]
        target[start:start + count] = source[...]
        start += count


def pick_rows(image_count, group):
    row = row_index(group)
    return one_hot(row // image_count * PAD + row % image_count, group // image_count * PAD)


def pick_kernel(image_count, values, grads_out, inputs_out):
    row = row_index(grads_out.shape[0])
    source = row // image_count * (2 * image_count) + row % image_count
    count = values.shape[0]
    grads_out[...] = dot(one_hot(source, count), values[...], NN).astype(BF16)
    inputs_out[...] = dot(one_hot(source + image_count, count), values[...], NN).astype(BF16)


def add_kernel(keep, arrived, keep_out, send_out):
    total = keep[...] + arrived[...].astype(F32)
    rows = keep_out.shape[0]
    keep_out[...], send_out[...] = total[:rows], total[rows:].astype(BF16)


def join_kernel(mine, arrived, sum_out):
    sum_out[...] = (mine[...] + arrived[...].astype(F32)).astype(BF16)


def spread_kernel(image_count, mine, other, spread_out):
    total = (mine[...] + other[...].astype(F32)).astype(BF16)
    spread_out[...] = dot(pick_rows(image_count, mine.shape[0]), total, TN).astype(BF16)


def expert_kernel(*refs):
    pre, w_out, w_in, act_out, grad_out, keep_out, send_out, grads = refs[-8:]
    stack(grads, refs[:-8])
    half = grads.shape[0] // 2
    for part in (0, 1):
        rows = slice(part * half, (part + 1) * half)
        hidden_grad = dot(grads[rows], w_out[...], NT)
        values = pre[rows].astype(F32)
        square = values * values
        bend = jnp.tanh(values * (SLOPE + SLOPE * CUBIC * square))
        step = 0.5 + 0.5 * bend
        act_out[rows] = (values * step).astype(BF16)
        slope = step + values * (0.5 - 0.5 * bend * bend) * (SLOPE + 3.0 * SLOPE * CUBIC * square)
        pre_grad = (hidden_grad * slope).astype(BF16)
        grad_out[rows] = pre_grad
        back = dot(pre_grad, w_in[...], NT)
        if part == 0:
            keep_out[...] = back
        else:
            send_out[...] = back.astype(BF16)


def out_weight_kernel(place, act_mine, act_other, *refs):
    keep_out, send_out, left, right = refs[-4:]
    stack(left, (act_mine, act_other))
    stack(right, refs[:-4])
    rows = keep_out.shape[0]
    zh0 = place[1]
    total = dot(left[...], right[...], TN)
    first, second = total[:rows], total[rows:]
    keep_out[...] = jnp.where(zh0 == 0, first, second)
    send_out[...] = jnp.where(zh0 == 0, second, first).astype(BF16)


def in_weight_kernel(place, grad_mine, grad_other, *refs):
    mine_out, pair_out, early_out, late_out, left, right, total = refs[-7:]
    stack(right, (grad_mine, grad_other))
    stack(left, refs[:-7])
    rows = mine_out.shape[0]
    position = place[0] * 2 + place[1]
    total[...] = dot(left[...], right[...], TN)

    def block(relative):
        return total[pl.ds(pl.multiple_of((position ^ relative) * rows, rows), rows)]

    mine_out[...], pair_out[...] = block(0), block(3)
    early_out[...], late_out[...] = block(2).astype(BF16), block(1).astype(BF16)


def sum_kernel(first, second, third, fourth, *outs):
    total = first[...].astype(F32) + second[...].astype(F32)
    total = total + (third[...].astype(F32) + fourth[...].astype(F32))
    for out in outs:
        out[...] = total.astype(out.dtype)


def local_call(kernel, outs, *operands, place=None, later_than=(), scratch=()):
    whole = pl.BlockSpec(memory_space=pltpu.VMEM)
    scalars = [] if place is None else [place]
    used = len(scalars) + len(operands)
    late = len(later_than)

    def body(*refs):
        kernel(*refs[:used], *refs[used + late:])

    return pl.pallas_call(
        body,
        out_shape=[jax.ShapeDtypeStruct(shape, dtype) for shape, dtype in outs],
        in_specs=[pl.BlockSpec(memory_space=pltpu.SMEM)] * len(scalars)
        + [whole] * len(operands)
        + [pl.BlockSpec(memory_space=pl.ANY)] * late,
        out_specs=[whole] * len(outs),
        scratch_shapes=[pltpu.VMEM(shape, dtype) for shape, dtype in scratch],
        compiler_params=pltpu.CompilerParams(vmem_limit_bytes=VMEM_LIMIT),
        cost_estimate=pl.CostEstimate(flops=0, bytes_accessed=0, transcendentals=0),
    )(*scalars, *operands, *later_than)


def swap(values, axis, mask):
    count = lax.axis_size(axis)
    return lax.ppermute(values, axis, [(k, k ^ mask) for k in range(count)])


def to_image_pair(values):
    return swap(values, IMG, 3)


def to_weight_pair(values):
    return swap(values, IMG, 1)


def flip_blocks(blocks):
    zh1, zh0 = lax.axis_index("zh1"), lax.axis_index("zh0")
    blocks = [jnp.where(zh0 == 0, blocks[k], blocks[k ^ 1]) for k in range(4)]
    return [jnp.where(zh1 == 0, blocks[k], blocks[k ^ 2]) for k in range(4)]


def sum_round(values, axes, dtype, later_than=()):
    moved = [swap(values, axes, mask) for mask in (1, 2, 3)]
    return local_call(
        sum_kernel, [(values.shape, dtype)], values, *moved, later_than=later_than
    )[0]


def share(values):
    joined = jnp.concatenate([values, swap(values, "yl", 1)])
    return joined, swap(joined, "c", 1)


def gather_share(keep, send):
    values = keep + swap(send, "c", 1).astype(F32)
    half = values.shape[0] // 2
    return values[:half] + swap(values[half:].astype(BF16), "yl", 1).astype(F32)


def on_device(tokens, router, grad_out, slot_out, hidden_pre, w_in, w_out):
    image_count, token_count, model_width = tokens.shape
    slot_count = router.shape[1]
    rows = image_count * token_count
    columns = slot_count * PAD
    group = slot_count * image_count
    zh1, zh0 = lax.axis_index("zh1"), lax.axis_index("zh0")
    place = jnp.stack([lax.axis_index(name) for name in ("zh1", "zh0", "yl", "c")])
    first_half = zh1 == 0

    hidden_pre = hidden_pre.reshape(-1, hidden_pre.shape[2])
    part = hidden_pre.shape[1] // 2
    w_in, w_out = w_in[0], w_out[0]
    share_rows = w_in.shape[0]
    w_in_mine = jnp.where(first_half, w_in[:, :part], w_in[:, part:])
    w_in_pair = to_image_pair(jnp.where(first_half, w_in[:, part:], w_in[:, :part]))
    half_rows = share_rows // 2
    cut = share_rows * 3 // 4
    w_out_early = to_weight_pair(w_out[:cut])
    mixed = jnp.concatenate(
        [w_out[cut:], jnp.concatenate([w_in_mine[:half_rows], w_in_mine[half_rows:]], axis=1)]
    )
    mixed = to_weight_pair(mixed)
    w_out_pair = jnp.concatenate([w_out_early, mixed[:share_rows - cut]])
    w_in_near = mixed[share_rows - cut:]
    w_in_near = jnp.concatenate([w_in_near[:, :part], w_in_near[:, part:]])
    pre_sent = jnp.where(first_half, hidden_pre[:, part:], hidden_pre[:, :part])
    early_rows = pre_sent.shape[0] * 2 // 3
    pre_early = to_image_pair(pre_sent[:early_rows])
    pre_late = to_image_pair(pre_sent[early_rows:])

    tokens = tokens.reshape(rows, model_width)
    grad_out = grad_out.reshape(rows, model_width)
    slots = ((columns, model_width), BF16)
    picked = ((group, model_width), BF16)
    wide = ((rows, columns), F32)
    slot_values, combine, dispatch = local_call(
        functools.partial(front_kernel, token_count),
        [((2 * group, model_width), BF16), wide, wide],
        tokens, grad_out, router,
    )
    slot_values_moved = lax.all_to_all(slot_values, EXPERT, 0, 0, tiled=True)
    (term,) = local_call(
        functools.partial(combine_kernel, slot_count), [wide],
        grad_out, slot_out.reshape(-1, model_width), combine,
        later_than=(slot_values,),
    )
    grads_own, inputs_own = local_call(
        functools.partial(pick_kernel, image_count), [picked, picked],
        slot_values_moved, later_than=(term, w_in_pair, w_out_early),
    )
    grads_pair = to_image_pair(grads_own)
    grads_mine = share(grads_own)
    inputs_mine = share(inputs_own)
    w_in_far = to_weight_pair(w_in_pair)
    half_pre = ((4 * group, part), BF16)
    (pre_mine,) = local_call(
        functools.partial(order_mine_kernel, image_count, group), [half_pre],
        hidden_pre,
        place=place, later_than=(grads_own,),
    )
    (grads_pair,) = local_call(
        pass_kernel, [picked], grads_pair,
        later_than=(pre_early, pre_mine, mixed, w_in_far, grads_mine[0], inputs_mine[0]),
    )
    grads_other = share(grads_pair)
    w_out_half = jnp.where(
        zh0 == 0, jnp.concatenate([w_out, w_out_pair]), jnp.concatenate([w_out_pair, w_out])
    )
    w_in_half = jnp.concatenate(
        flip_blocks([w_in_mine, w_in_near, w_in_far, w_in_pair])
    )
    expert_outs = [
        ((4 * group, part), BF16),
        ((4 * group, part), BF16),
        ((2 * group, model_width), F32),
        ((2 * group, model_width), BF16),
    ]
    expert_scratch = [((4 * group, model_width), BF16)]
    act_mine, pre_grad_mine, keep_mine, send_mine = local_call(
        expert_kernel, expert_outs,
        *grads_mine, pre_mine, w_out_half, w_in_half,
        later_than=(grads_other[0],), scratch=expert_scratch,
    )
    (pre_other,) = local_call(
        functools.partial(order_other_kernel, image_count, group), [half_pre],
        pre_early, pre_late,
        place=place, later_than=(act_mine,),
    )
    act_other, pre_grad_other, keep_other, send_other = local_call(
        expert_kernel, expert_outs,
        *grads_other, pre_other, w_out_half, w_in_half,
        later_than=(act_mine,), scratch=expert_scratch,
    )
    back_mine = gather_share(keep_mine, send_mine)
    out_keep, out_sent = local_call(
        out_weight_kernel,
        [((share_rows, model_width), F32), ((share_rows, model_width), BF16)],
        act_mine, act_other, *grads_mine, *grads_other,
        place=place, later_than=(send_other,),
        scratch=[((8 * group, part), BF16), ((8 * group, model_width), BF16)],
    )
    out_arrived = to_weight_pair(out_sent)

    (inputs_sent,) = local_call(pass_kernel, [picked], inputs_own, later_than=(pre_late,))
    inputs_pair = to_image_pair(inputs_sent)

    half_sum, half_sent = local_call(
        add_kernel, [((group, model_width), F32), picked],
        keep_other, swap(send_other, "c", 1), later_than=(out_keep,),
    )
    (back_other,) = local_call(
        join_kernel, [picked],
        half_sum, swap(half_sent, "yl", 1), later_than=(inputs_pair,),
    )
    back_pair = to_image_pair(back_other)
    (inputs_pair,) = local_call(
        pass_kernel, [picked], inputs_pair, later_than=(back_other,)
    )
    (inputs_joined,) = local_call(
        stack_kernel, [((2 * group, model_width), BF16)],
        inputs_pair, swap(inputs_pair, "yl", 1), later_than=(back_pair,),
    )
    inputs_other = inputs_joined, swap(inputs_joined, "c", 1)

    in_mine, in_pair, in_early, in_late = local_call(
        in_weight_kernel,
        [((share_rows, part), F32)] * 2 + [((share_rows, part), BF16)] * 2,
        pre_grad_mine, pre_grad_other, *inputs_mine, *inputs_other,
        place=place, later_than=(out_keep,),
        scratch=[
            ((8 * group, model_width), BF16), ((8 * group, part), BF16), ((model_width, part), F32),
        ],
    )
    in_early = to_weight_pair(in_early)
    (back,) = local_call(
        functools.partial(spread_kernel, image_count), [slots],
        back_mine, back_pair, later_than=(out_arrived,),
    )
    input_grads = lax.all_to_all(back, EXPERT, 0, 0, tiled=True)
    logit_grads, router_grads = local_call(
        functools.partial(logit_kernel, token_count, slot_count),
        [((rows, columns), BF16), ((slot_count, model_width), F32)],
        tokens, dispatch, term, input_grads, later_than=(in_mine,),
    )
    (token_grads,) = local_call(
        token_kernel, [((rows, model_width), BF16)],
        dispatch, logit_grads, router, input_grads,
    )
    (in_pair_sum,) = local_call(join_kernel, [((share_rows, part), BF16)], in_pair, in_early)
    (in_late,) = local_call(
        pass_kernel, [((share_rows, part), BF16)], in_late, later_than=(in_pair_sum,)
    )
    in_late = to_weight_pair(in_late)
    in_pair = to_image_pair(in_pair_sum)
    router_sum = sum_round(router_grads, ("yl", "c"), F32, later_than=(token_grads,))
    router_sum = sum_round(router_sum, ("x",), BF16, later_than=(in_pair_sum,))
    router_sum = sum_round(router_sum, ("zl", "yh"), BF16, later_than=(in_pair,))
    router_sum = sum_round(router_sum, IMG, F32)
    (in_mine,) = local_call(join_kernel, [((share_rows, part), BF16)], in_mine, in_late)
    out_gradient = (out_keep + out_arrived.astype(F32)).astype(BF16)
    in_gradient = jnp.where(
        first_half,
        jnp.concatenate([in_mine, in_pair], axis=1),
        jnp.concatenate([in_pair, in_mine], axis=1),
    )
    return (
        token_grads.reshape(image_count, token_count, model_width),
        in_gradient[None],
        out_gradient[None],
        router_sum.T,
    )


def solution(mesh):
    fine = Mesh(mesh.devices.reshape(2, 2, 4, 2, 2, 2, 2), AXES)
    in_specs = (
        P(AXES, None, None),
        P(),
        P(AXES, None, None),
        P(AXES, None, None),
        P(IMG, EXP, None),
        P(EXP, IMG, None),
        P(EXP, IMG, None),
    )
    out_specs = (P(AXES, None, None), P(EXP, IMG, None), P(EXP, IMG, None), P())
    return jax.shard_map(
        on_device, mesh=fine, in_specs=in_specs, out_specs=out_specs, check_vma=False
    )
```

```python
import functools

import jax
import jax.numpy as jnp
from jax import lax
from jax.experimental import pallas as pl
from jax.experimental.pallas import tpu as pltpu
from jax.sharding import Mesh, PartitionSpec as P

BF16 = jnp.bfloat16
F32 = jnp.float32
IMG = ("zh1", "zh0")
EXP = ("x", "zl", "yh", "yl", "c")
AXES = IMG + EXP
EXPERT = ("x", "zl", "yh")
PAD = 16
VMEM_LIMIT = 26 * 1024 * 1024
CUBIC = 0.044715
SLOPE = 0.7978845608028654


def dot(a, b, dims):
    return lax.dot_general(a, b, (dims, ((), ())), preferred_element_type=F32)


NN = ((1,), (0,))
NT = ((1,), (1,))
TN = ((0,), (0,))


def row_index(count):
    return lax.broadcasted_iota(jnp.int32, (count, 1), 0)


def one_hot(wanted, width):
    return (lax.broadcasted_iota(jnp.int32, (wanted.shape[0], width), 1) == wanted).astype(BF16)


def own_image(rows, columns, token_count):
    image = lax.broadcasted_iota(jnp.int32, (1, columns), 1) % PAD
    return row_index(rows) // token_count == image


def widen(router):
    slot_count = router.shape[1]
    slot = lax.broadcasted_iota(jnp.int32, (slot_count, slot_count * PAD), 0)
    column = lax.broadcasted_iota(jnp.int32, (slot_count, slot_count * PAD), 1)
    return dot(router[...], (column // PAD == slot).astype(BF16), NN).astype(BF16)


def spread_columns(columns, width, image_count, start):
    row = row_index(columns)
    column = row // PAD * (2 * image_count) + row % PAD + start
    return one_hot(jnp.where(row % PAD < image_count, column, width), width)


def front_kernel(token_count, tokens, grad_out, router, slots_out, combine_out, dispatch_out):
    rows, columns = combine_out.shape
    image_count = rows // token_count
    width = slots_out.shape[0]
    logits = dot(tokens[...], widen(router), NN)
    mine = own_image(rows, columns, token_count)
    weights = jnp.exp(logits - jnp.max(logits, axis=1, keepdims=True))
    weights = jnp.where(mine, weights, 0.0)
    combine = weights / jnp.sum(weights, axis=1, keepdims=True)
    weights = dot(combine.astype(BF16), spread_columns(columns, width, image_count, 0), NN)
    slots = dot(weights.astype(BF16), grad_out[...], TN)
    combine_out[...] = combine
    by_image = logits.reshape(rows // token_count, token_count, columns)
    weights = jnp.exp(by_image - jnp.max(by_image, axis=1, keepdims=True))
    dispatch = weights / jnp.sum(weights, axis=1, keepdims=True)
    dispatch = jnp.where(mine, dispatch.reshape(rows, columns), 0.0)
    order = spread_columns(columns, width, image_count, image_count)
    weights = dot(dispatch.astype(BF16), order, NN)
    slots_out[...] = (slots + dot(weights.astype(BF16), tokens[...], TN)).astype(BF16)
    dispatch_out[...] = dispatch


def combine_kernel(slot_count, grad_out, slot_out, combine, term_out):
    row = row_index(combine.shape[1])
    order = one_hot(row % PAD * slot_count + row // PAD, slot_out.shape[0])
    order = jnp.where(row % PAD < slot_out.shape[0] // slot_count, order, jnp.zeros_like(order))
    outputs = dot(order, slot_out[...], NN).astype(BF16)
    weights = combine[...]
    grads = weights * dot(grad_out[...], outputs, NT)
    term_out[...] = grads - weights * jnp.sum(grads, axis=1, keepdims=True)


def logit_kernel(token_count, slot_count, tokens, dispatch, term, input_grads, logit_out, router_out):
    rows, columns = dispatch.shape
    images = rows // token_count
    weights = dispatch[...]
    grads = weights * dot(tokens[...], input_grads[...], NT)
    total = jnp.sum(grads.reshape(images, token_count, columns), axis=1, keepdims=True)
    total = jnp.broadcast_to(total, (images, token_count, columns)).reshape(rows, columns)
    logit_grads = (grads - weights * total + term[...]).astype(BF16)
    logit_out[...] = logit_grads
    fold = one_hot(row_index(columns) // PAD, slot_count)
    by_slot = dot(logit_grads, fold, NN).astype(BF16)
    router_out[...] = dot(by_slot, tokens[...], TN).astype(router_out.dtype)


def token_kernel(dispatch, logit_grads, router, input_grads, tokens_out):
    total = dot(logit_grads[...], widen(router), NT)
    total = total + dot(dispatch[...].astype(BF16), input_grads[...], NN)
    tokens_out[...] = total.astype(BF16)


def orders(image_count, group, place, count):
    row = row_index(group)
    base = row // image_count * (4 * image_count) + row % image_count
    for piece in range(4):
        member = ((piece % 2) ^ place[2]) * 2 + ((piece // 2) ^ place[3])
        rows = slice(piece * group, (piece + 1) * group)
        yield rows, one_hot(base + member * image_count, count)


def order_mine_kernel(image_count, group, place, hidden_pre, mine_out):
    half = mine_out.shape[1]
    values = jnp.where(place[0] == 0, hidden_pre[:, :half], hidden_pre[:, half:])
    for rows, order in orders(image_count, group, place, hidden_pre.shape[0]):
        mine_out[rows] = dot(order, values, NN).astype(BF16)


def order_other_kernel(image_count, group, place, first, second, other_out):
    count = first.shape[0]
    for rows, order in orders(image_count, group, place, count + second.shape[0]):
        other = dot(order[:, :count], first[...], NN) + dot(order[:, count:], second[...], NN)
        other_out[rows] = other.astype(BF16)


def pass_kernel(values, values_out):
    values_out[...] = values[:values_out.shape[0]]


def stack_kernel(first, second, stacked_out):
    stack(stacked_out, (first, second))


def stack(target, sources):
    start = 0
    for source in sources:
        count = source.shape[0]
        target[start:start + count] = source[...]
        start += count


def pick_rows(image_count, group):
    row = row_index(group)
    return one_hot(row // image_count * PAD + row % image_count, group // image_count * PAD)


def pick_kernel(image_count, values, grads_out, inputs_out):
    row = row_index(grads_out.shape[0])
    source = row // image_count * (2 * image_count) + row % image_count
    count = values.shape[0]
    grads_out[...] = dot(one_hot(source, count), values[...], NN).astype(BF16)
    inputs_out[...] = dot(one_hot(source + image_count, count), values[...], NN).astype(BF16)


def add_kernel(keep, arrived, keep_out, send_out):
    total = keep[...] + arrived[...].astype(F32)
    rows = keep_out.shape[0]
    keep_out[...], send_out[...] = total[:rows], total[rows:].astype(BF16)


def join_kernel(mine, arrived, sum_out):
    sum_out[...] = (mine[...].astype(F32) + arrived[...].astype(F32)).astype(BF16)


def spread_kernel(image_count, mine, other, spread_out):
    total = (mine[...] + other[...].astype(F32)).astype(BF16)
    spread_out[...] = dot(pick_rows(image_count, mine.shape[0]), total, TN).astype(BF16)


def expert_kernel(*refs):
    *grads, pre, w_out, w_in, act_out, grad_out, keep_out, send_out = refs
    half = grads[0].shape[0]
    for part in (0, 1):
        rows = slice(part * half, (part + 1) * half)
        hidden_grad = dot(grads[part][...], w_out[...], NT)
        values = pre[rows].astype(F32)
        square = values * values
        bend = jnp.tanh(values * (SLOPE + SLOPE * CUBIC * square))
        step = 0.5 + 0.5 * bend
        act_out[rows] = (values * step).astype(BF16)
        slope = step + values * (0.5 - 0.5 * bend * bend) * (SLOPE + 3.0 * SLOPE * CUBIC * square)
        pre_grad = (hidden_grad * slope).astype(BF16)
        grad_out[rows] = pre_grad
        back = dot(pre_grad, w_in[...], NT)
        if part == 0:
            keep_out[...] = back
        else:
            send_out[...] = back.astype(BF16)


def out_weight_kernel(place, act_mine, act_other, *refs):
    keep_out, send_out, left, right = refs[-4:]
    stack(left, (act_mine, act_other))
    stack(right, refs[:-4])
    rows = keep_out.shape[0]
    zh0 = place[1]
    total = dot(left[...], right[...], TN)
    first, second = total[:rows], total[rows:]
    keep_out[...] = jnp.where(zh0 == 0, first, second).astype(BF16)
    send_out[...] = jnp.where(zh0 == 0, second, first).astype(BF16)


def in_weight_kernel(place, grad_mine, grad_other, *refs):
    mine_out, pair_out, early_out, late_out, left, right, total = refs[-7:]
    stack(right, (grad_mine, grad_other))
    stack(left, refs[:-7])
    rows = mine_out.shape[0]
    position = place[0] * 2 + place[1]
    total[...] = dot(left[...], right[...], TN).astype(BF16)

    def block(relative):
        return total[pl.ds(pl.multiple_of((position ^ relative) * rows, rows), rows)]

    mine_out[...], pair_out[...] = block(0), block(3)
    early_out[...], late_out[...] = block(2), block(1)


def sum_kernel(first, second, third, fourth, *outs):
    total = first[...].astype(F32) + second[...].astype(F32)
    total = total + (third[...].astype(F32) + fourth[...].astype(F32))
    for out in outs:
        out[...] = total.astype(out.dtype)


def local_call(kernel, outs, *operands, place=None, later_than=(), scratch=()):
    whole = pl.BlockSpec(memory_space=pltpu.VMEM)
    scalars = [] if place is None else [place]
    used = len(scalars) + len(operands)
    late = len(later_than)

    def body(*refs):
        kernel(*refs[:used], *refs[used + late:])

    return pl.pallas_call(
        body,
        out_shape=[jax.ShapeDtypeStruct(shape, dtype) for shape, dtype in outs],
        in_specs=[pl.BlockSpec(memory_space=pltpu.SMEM)] * len(scalars)
        + [whole] * len(operands)
        + [pl.BlockSpec(memory_space=pl.ANY)] * late,
        out_specs=[whole] * len(outs),
        scratch_shapes=[pltpu.VMEM(shape, dtype) for shape, dtype in scratch],
        compiler_params=pltpu.CompilerParams(vmem_limit_bytes=VMEM_LIMIT),
        cost_estimate=pl.CostEstimate(flops=0, bytes_accessed=0, transcendentals=0),
    )(*scalars, *operands, *later_than)


def swap(values, axis, mask):
    count = lax.axis_size(axis)
    return lax.ppermute(values, axis, [(k, k ^ mask) for k in range(count)])


def to_image_pair(values):
    return swap(values, IMG, 3)


def to_weight_pair(values):
    return swap(values, IMG, 1)


def flip_blocks(blocks):
    zh1, zh0 = lax.axis_index("zh1"), lax.axis_index("zh0")
    blocks = [jnp.where(zh0 == 0, blocks[k], blocks[k ^ 1]) for k in range(4)]
    return [jnp.where(zh1 == 0, blocks[k], blocks[k ^ 2]) for k in range(4)]


def sum_round(values, axes, dtype, later_than=()):
    moved = [swap(values, axes, mask) for mask in (1, 2, 3)]
    return local_call(
        sum_kernel, [(values.shape, dtype)], values, *moved, later_than=later_than
    )[0]


def share(values):
    joined = jnp.concatenate([values, swap(values, "yl", 1)])
    return joined, swap(joined, "c", 1)


def gather_share(keep, send):
    values = keep + swap(send, "c", 1).astype(F32)
    half = values.shape[0] // 2
    return values[:half] + swap(values[half:].astype(BF16), "yl", 1).astype(F32)


def on_device(tokens, router, grad_out, slot_out, hidden_pre, w_in, w_out):
    image_count, token_count, model_width = tokens.shape
    slot_count = router.shape[1]
    rows = image_count * token_count
    columns = slot_count * PAD
    group = slot_count * image_count
    zh1, zh0 = lax.axis_index("zh1"), lax.axis_index("zh0")
    place = jnp.stack([lax.axis_index(name) for name in ("zh1", "zh0", "yl", "c")])
    first_half = zh1 == 0

    hidden_pre = hidden_pre.reshape(-1, hidden_pre.shape[2])
    part = hidden_pre.shape[1] // 2
    w_in, w_out = w_in[0], w_out[0]
    share_rows = w_in.shape[0]
    w_in_mine = jnp.where(first_half, w_in[:, :part], w_in[:, part:])
    w_in_pair = to_image_pair(jnp.where(first_half, w_in[:, part:], w_in[:, :part]))
    half_rows = share_rows // 2
    cut = share_rows * 3 // 4
    w_out_early = to_weight_pair(w_out[:cut])
    mixed = jnp.concatenate(
        [w_out[cut:], jnp.concatenate([w_in_mine[:half_rows], w_in_mine[half_rows:]], axis=1)]
    )
    mixed = to_weight_pair(mixed)
    w_out_pair = jnp.concatenate([w_out_early, mixed[:share_rows - cut]])
    w_in_near = mixed[share_rows - cut:]
    w_in_near = jnp.concatenate([w_in_near[:, :part], w_in_near[:, part:]])
    pre_sent = jnp.where(first_half, hidden_pre[:, part:], hidden_pre[:, :part])
    early_rows = pre_sent.shape[0] * 2 // 3
    pre_early = to_image_pair(pre_sent[:early_rows])
    pre_late = to_image_pair(pre_sent[early_rows:])

    tokens = tokens.reshape(rows, model_width)
    grad_out = grad_out.reshape(rows, model_width)
    slots = ((columns, model_width), BF16)
    picked = ((group, model_width), BF16)
    wide = ((rows, columns), F32)
    slot_values, combine, dispatch = local_call(
        functools.partial(front_kernel, token_count),
        [((2 * group, model_width), BF16), wide, wide],
        tokens, grad_out, router,
    )
    slot_values_moved = lax.all_to_all(slot_values, EXPERT, 0, 0, tiled=True)
    (term,) = local_call(
        functools.partial(combine_kernel, slot_count), [wide],
        grad_out, slot_out.reshape(-1, model_width), combine,
        later_than=(slot_values,),
    )
    grads_own, inputs_own = local_call(
        functools.partial(pick_kernel, image_count), [picked, picked],
        slot_values_moved, later_than=(term, w_in_pair, w_out_early),
    )
    grads_pair = to_image_pair(grads_own)
    grads_mine = share(grads_own)
    inputs_mine = share(inputs_own)
    w_in_far = to_weight_pair(w_in_pair)
    half_pre = ((4 * group, part), BF16)
    (pre_mine,) = local_call(
        functools.partial(order_mine_kernel, image_count, group), [half_pre],
        hidden_pre,
        place=place, later_than=(grads_own,),
    )
    w_out_half = jnp.where(
        zh0 == 0, jnp.concatenate([w_out, w_out_pair]), jnp.concatenate([w_out_pair, w_out])
    )
    w_in_half = jnp.concatenate(
        flip_blocks([w_in_mine, w_in_near, w_in_far, w_in_pair])
    )
    (grads_pair,) = local_call(
        pass_kernel, [picked], grads_pair,
        later_than=(pre_early, pre_mine, mixed, w_in_far, grads_mine[0], inputs_mine[0]),
    )
    grads_other = share(grads_pair)
    expert_outs = [
        ((4 * group, part), BF16),
        ((4 * group, part), BF16),
        ((2 * group, model_width), F32),
        ((2 * group, model_width), BF16),
    ]
    act_mine, pre_grad_mine, keep_mine, send_mine = local_call(
        expert_kernel, expert_outs,
        *grads_mine, pre_mine, w_out_half, w_in_half,
        later_than=(grads_other[0],),
    )
    (pre_other,) = local_call(
        functools.partial(order_other_kernel, image_count, group), [half_pre],
        pre_early, pre_late,
        place=place, later_than=(act_mine,),
    )
    act_other, pre_grad_other, keep_other, send_other = local_call(
        expert_kernel, expert_outs,
        *grads_other, pre_other, w_out_half, w_in_half,
        later_than=(act_mine,),
    )
    back_mine = gather_share(keep_mine, send_mine)
    out_keep, out_sent = local_call(
        out_weight_kernel,
        [((share_rows, model_width), BF16)] * 2,
        act_mine, act_other, *grads_mine, *grads_other,
        place=place, later_than=(send_other,),
        scratch=[((8 * group, part), BF16), ((8 * group, model_width), BF16)],
    )
    out_arrived = to_weight_pair(out_sent)

    (inputs_sent,) = local_call(pass_kernel, [picked], inputs_own, later_than=(pre_late,))
    inputs_pair = to_image_pair(inputs_sent)

    half_sum, half_sent = local_call(
        add_kernel, [((group, model_width), F32), picked],
        keep_other, swap(send_other, "c", 1), later_than=(out_keep,),
    )
    (back_other,) = local_call(
        join_kernel, [picked],
        half_sum, swap(half_sent, "yl", 1),
    )
    back_pair = to_image_pair(back_other)
    (inputs_pair,) = local_call(
        pass_kernel, [picked], inputs_pair, later_than=(back_other,)
    )
    (inputs_joined,) = local_call(
        stack_kernel, [((2 * group, model_width), BF16)],
        inputs_pair, swap(inputs_pair, "yl", 1),
    )
    inputs_other = inputs_joined, swap(inputs_joined, "c", 1)

    in_mine, in_pair, in_early, in_late = local_call(
        in_weight_kernel,
        [((share_rows, part), BF16)] * 4,
        pre_grad_mine, pre_grad_other, *inputs_mine, *inputs_other,
        place=place, later_than=(out_keep,),
        scratch=[
            ((8 * group, model_width), BF16), ((8 * group, part), BF16), ((model_width, part), BF16),
        ],
    )
    in_early = to_weight_pair(in_early)
    (back,) = local_call(
        functools.partial(spread_kernel, image_count), [slots],
        back_mine, back_pair, later_than=(out_arrived, inputs_joined),
    )
    input_grads = lax.all_to_all(back, EXPERT, 0, 0, tiled=True)
    logit_grads, router_grads = local_call(
        functools.partial(logit_kernel, token_count, slot_count),
        [((rows, columns), BF16), ((slot_count, model_width), F32)],
        tokens, dispatch, term, input_grads, later_than=(in_mine,),
    )
    (token_grads,) = local_call(
        token_kernel, [((rows, model_width), BF16)],
        dispatch, logit_grads, router, input_grads,
    )
    (in_pair_sum,) = local_call(join_kernel, [((share_rows, part), BF16)], in_pair, in_early)
    (in_late,) = local_call(
        pass_kernel, [((share_rows, part), BF16)], in_late, later_than=(in_pair_sum,)
    )
    in_late = to_weight_pair(in_late)
    in_pair = to_image_pair(in_pair_sum)
    router_sum = sum_round(router_grads, ("yl", "c"), F32, later_than=(token_grads,))
    router_sum = sum_round(router_sum, ("x",), BF16, later_than=(in_pair_sum,))
    router_sum = sum_round(router_sum, ("zl", "yh"), BF16, later_than=(in_pair,))
    router_sum = sum_round(router_sum, IMG, F32)
    (in_mine,) = local_call(join_kernel, [((share_rows, part), BF16)], in_mine, in_late)
    out_gradient = (out_keep.astype(F32) + out_arrived.astype(F32)).astype(BF16)
    in_gradient = jnp.where(
        first_half,
        jnp.concatenate([in_mine, in_pair], axis=1),
        jnp.concatenate([in_pair, in_mine], axis=1),
    )
    return (
        token_grads.reshape(image_count, token_count, model_width),
        in_gradient[None],
        out_gradient[None],
        router_sum.T,
    )


def solution(mesh):
    fine = Mesh(mesh.devices.reshape(2, 2, 4, 2, 2, 2, 2), AXES)
    in_specs = (
        P(AXES, None, None),
        P(),
        P(AXES, None, None),
        P(AXES, None, None),
        P(IMG, EXP, None),
        P(EXP, IMG, None),
        P(EXP, IMG, None),
    )
    out_specs = (P(AXES, None, None), P(EXP, IMG, None), P(EXP, IMG, None), P())
    return jax.shard_map(
        on_device, mesh=fine, in_specs=in_specs, out_specs=out_specs, check_vma=False
    )
```
